256 devices in a mesh: leaf: 16 (over x, y), row: 16 (over z, core).
Axes of the slice: x: 4, y: 4, z: 8, core: 2. Of those that a mesh axis runs over, the one named last changes fastest.
Arguments:
- rhs: bfloat16 [6, 16, 512, 256], P(None, 'leaf', 'row'), may hold values from -6 to 6
- diag_inverse: bfloat16 [16, 6, 512, 512], P('leaf'), as said below
- factor: bfloat16 [16, 178, 512, 512], P('leaf', None, 'row'), as said below
- widths: int32 [6, 16], P(None, 'leaf'), may hold values from 64 to 512, as said below
- structure: int32 [16, 178], P('leaf'), may hold values from 0 to 1, as said below
Outputs:
- forward_solution: bfloat16 [6, 16, 512, 256], P(None, 'leaf', 'row')
- adjoint_solution: bfloat16 [6, 16, 512, 256], P(None, 'leaf', 'row')
The draws below stay inside these ranges and needn't reach their ends.
Inputs may be any that keep to these rules, and one draw needn't show every extreme that they name: `widths`: every draw has a supernode of exactly 512 columns and one of exactly one eighth of 512 columns. `structure`: 1 where the block is present. Each diag_inverse[j, l] is lower triangular with diagonal entries from 0.5 to 1. `factor`: dense blocks of independent entries.
All inputs are finite; a program needn't handle non-finite values.
Results may differ from the reference program's by a relative error of at most 0.017.
Values may be sent and summed in bfloat16 or wider, within the bound.
A program may use at most 64 MiB of HBM per device.

```python
import math
import jax
import jax.numpy as jnp
import numpy as np
from jax import lax

W = 512
RHS = 256
LEVELS = 6
BLOCKS = 178
N_LEAF = 16


def factor_scales():
    values = []
    for source_level in range(LEVELS):
        for target_level in range(source_level + 1, LEVELS):
            group_span = min(2 ** target_level, N_LEAF)
            values = values + [1.0 / math.sqrt(W * target_level * group_span)] * group_span
    return np.array(values, dtype=np.float32)


def draw_factor(key, part):
    scales = jnp.asarray(factor_scales())

    def one_leaf(leaf_number):
        leaf_key = jax.random.fold_in(key, leaf_number)
        base_draw = jax.random.truncated_normal(leaf_key, -4.0, 4.0, (BLOCKS, W, W), jnp.float32)
        return (base_draw * scales[:, None, None]).astype(jnp.bfloat16)
    return lax.map(one_leaf, jnp.arange(N_LEAF))


def draw_diag_inverse(key, part):
    positions = jnp.arange(W)
    strict = (positions[None, :] < positions[:, None]).astype(jnp.float32)
    identity = (positions[None, :] == positions[:, None]).astype(jnp.float32)

    def one_leaf(leaf_number):
        key_lower, key_diagonal = jax.random.split(jax.random.fold_in(key, leaf_number))
        lower_part = jax.random.truncated_normal(key_lower, -4.0, 4.0, (LEVELS, W, W), jnp.float32)
        diagonal = jax.random.uniform(key_diagonal, (LEVELS, W, 1), jnp.float32, 0.5, 1.0)
        matrix = lower_part * strict * math.sqrt(0.5 / W) + identity * diagonal
        return matrix.astype(jnp.bfloat16)
    return lax.map(one_leaf, jnp.arange(N_LEAF))


def draw_widths(key, part):
    entries = LEVELS * N_LEAF
    key_values, key_wide, key_narrow = jax.random.split(key, 3)
    values = jax.random.randint(key_values, (entries,), W // 8, W + 1)
    widest = jax.random.randint(key_wide, (), 0, entries)
    narrow = (widest + jax.random.randint(key_narrow, (), 1, entries)) % entries
    positions = jnp.arange(entries)
    values = jnp.where(positions == widest, W, values)
    values = jnp.where(positions == narrow, W // 8, values)
    return values.reshape(LEVELS, N_LEAF).astype(jnp.int32)


def draw_structure(key, part):
    key_density, key_entries = jax.random.split(key)
    density = jax.random.randint(key_density, (N_LEAF, 1), 1, 9)
    entries = jax.random.randint(key_entries, (N_LEAF, BLOCKS), 0, 8)
    return (entries < density).astype(jnp.int32)


def levels(key, dims, shards, smallest, high):
    loudness = 1.0
    for dim, parts in shards:
        draws = jax.random.uniform(jax.random.fold_in(jax.random.fold_in(key, 6), dim), (parts,), jnp.float32, smallest / len(shards), high / len(shards))
        loudness = loudness * jnp.repeat(jnp.exp(draws), dims[dim] // parts).reshape((-1,) + (1,) * (len(dims) - 1 - dim))
    return loudness


def scatter_about(own_key, extent, width, reach, cuts=(), held_as=jnp.bfloat16):
    level = levels(own_key, extent, cuts, -0.22, 0.18) if cuts else 1.0
    drawn = jax.random.normal(own_key, extent, jnp.float32) * width * level
    return jnp.minimum(jnp.maximum(drawn, -reach), reach).astype(held_as)


def setup_inputs(seed: int = 0) -> dict:
    keys = jax.random.split(jax.random.key(seed), 6)
    return {
        "rhs": scatter_about(keys[0], (LEVELS, N_LEAF, W, RHS), 1.0, 6.0, ((1, 16), (2, 16))),
        "diag_inverse": draw_diag_inverse(jax.random.fold_in(keys[5], 71), 0),
        "factor": draw_factor(jax.random.fold_in(keys[5], 71), 0),
        "widths": draw_widths(jax.random.fold_in(keys[5], 71), 0),
        "structure": draw_structure(jax.random.fold_in(keys[5], 71), 0),
    }


def group_size(level_now):
    return min(2 ** level_now, N_LEAF)


def block_offsets():
    offset_table = {}
    cursor = 0
    for source_level in range(LEVELS):
        for target_level in range(source_level + 1, LEVELS):
            offset_table[(source_level, target_level)] = cursor
            cursor += group_size(target_level)
    return offset_table


def push_block(items):
    block_group, weight_row, values = items
    product = jnp.einsum("mrc,cn->mrn", block_group.astype(jnp.float32), values.astype(jnp.float32), precision=lax.Precision.HIGHEST)
    return product * weight_row[:, None, None]


def pull_block(items):
    block_group, weight_row, values = items
    weighted = values.astype(jnp.float32) * weight_row[:, None, None]
    return jnp.einsum("mrc,mrn->cn", block_group.astype(jnp.float32), weighted, precision=lax.Precision.HIGHEST)


def reference(rhs, diag_inverse, factor, widths, structure):
    offset_table = block_offsets()
    positions = jnp.arange(W, dtype=jnp.int32)
    row_masks = (positions[None, None, :] < widths[:, :, None]).astype(jnp.float32)[..., None]
    weights = structure.astype(jnp.float32)
    forward = []
    for level_now in range(LEVELS):
        group_span = group_size(level_now)
        updates = jnp.zeros((N_LEAF, W, RHS), jnp.float32)
        for source_level in range(level_now):
            first_block = offset_table[(source_level, level_now)]
            pushed = lax.map(push_block, (factor[:, first_block:first_block + group_span], weights[:, first_block:first_block + group_span], forward[source_level]))
            pushed = pushed.reshape(N_LEAF // group_span, group_span, group_span, W, RHS).sum(axis=1)
            updates = updates + pushed.reshape(N_LEAF, W, RHS)
        residual = (row_masks[level_now] * (rhs[level_now].astype(jnp.float32) - updates)).astype(jnp.bfloat16)
        inverse = diag_inverse[:, level_now].astype(jnp.float32)
        solved = jnp.einsum("irc,icn->irn", inverse, residual.astype(jnp.float32), precision=lax.Precision.HIGHEST)
        forward.append((row_masks[level_now] * solved).astype(jnp.bfloat16))
    adjoint = [None] * LEVELS
    for level_now in reversed(range(LEVELS)):
        pulled = jnp.zeros((N_LEAF, W, RHS), jnp.float32)
        for target_level in range(level_now + 1, LEVELS):
            group_span = group_size(target_level)
            first_block = offset_table[(level_now, target_level)]
            grouped = adjoint[target_level].reshape(N_LEAF // group_span, 1, group_span, W, RHS)
            per_source = jnp.broadcast_to(grouped, (N_LEAF // group_span, group_span, group_span, W, RHS)).reshape(N_LEAF, group_span, W, RHS)
            pulled = pulled + lax.map(pull_block, (factor[:, first_block:first_block + group_span], weights[:, first_block:first_block + group_span], per_source))
        reduced = (row_masks[level_now] * (forward[level_now].astype(jnp.float32) - pulled)).astype(jnp.bfloat16)
        inverse = diag_inverse[:, level_now].astype(jnp.float32)
        solved = jnp.einsum("icr,icn->irn", inverse, reduced.astype(jnp.float32), precision=lax.Precision.HIGHEST)
        adjoint[level_now] = (row_masks[level_now] * solved).astype(jnp.bfloat16)
    return jnp.stack(forward), jnp.stack(adjoint)
```

```python
import functools
import jax
import jax.numpy as jnp
from jax import lax
from jax.experimental import pallas as pl
from jax.experimental.pallas import tpu as pltpu
from jax.sharding import PartitionSpec as P

MESH = pl.DeviceIdType.MESH
F32 = jnp.float32
BF16 = jnp.bfloat16
LEVELS = 6
LEAVES = 16
ROWS = 32
WIDTH = 512
COLUMNS = 256
STREAMS = 1
PART = COLUMNS // STREAMS
TARGETS = tuple(range(1, LEVELS))


def group_size(level):
    return min(2**level, LEAVES)


def block_offsets():
    table, cursor = {}, 0
    for source in range(LEVELS):
        for target in range(source + 1, LEVELS):
            table[source, target] = cursor
            cursor += group_size(target)
    return table


OFFSETS = block_offsets()
BLOCKS = sum(group_size(t) * t for t in TARGETS)


def dot(a, b):
    return jnp.dot(a, b, preferred_element_type=F32)


def dot_nt(a, b):
    return lax.dot_general(a, b, (((1,), (1,)), ((), ())), preferred_element_type=F32)


ROW_Z, ROW_SIB, LEAF, B_LEAF, B_SIB, B_Z = (i * LEVELS for i in range(6))
SLOTS = 6 * LEVELS


def kernel(rhs, diag, factor, widths, structure, fwd, adj, *scratch):
    scratch = list(scratch)

    def take(n):
        out = scratch[:n]
        del scratch[:n]
        return out

    per_target = lambda: dict(zip(TARGETS, take(len(TARGETS))))
    blocks, fold, fold_t = per_target(), per_target(), per_target()
    dm, dm_t, twice = take(3)
    pre, part_out, part_in = per_target(), per_target(), per_target()
    resid = take(1)[0]
    gathered = per_target()
    pulled_pre, pulled_out, pulled_sib, pair_out, pair_in, head = take(6)
    send_sem, recv_sem, load_sem = take(3)

    leaf = lax.axis_index("leaf")
    row = lax.axis_index("row")
    z, core = row // 2, lax.rem(row, 2)
    sibling = z * 2 + (1 - core)
    other = 1 - core
    own = pl.ds(pl.multiple_of(row * ROWS, ROWS), ROWS)

    diag_load = pltpu.make_async_copy(diag.at[0], dm, load_sem.at[0])
    diag_load.start()
    loads = {}
    for i, t in enumerate(TARGETS):
        for s in range(t):
            loads[s, t] = pltpu.make_async_copy(
                factor.at[0, pl.ds(OFFSETS[s, t], group_size(t))],
                blocks[t].at[s],
                load_sem.at[1 + len(loads)],
            )
            loads[s, t].start()

    barrier = pltpu.get_barrier_semaphore()

    def greet(leaf_to, row_to):
        pl.semaphore_signal(barrier, inc=1, device_id=(leaf_to, row_to), device_id_type=MESH)

    for k in range(1, LEAVES):
        greet(lax.rem(leaf + k, LEAVES), row)
    for k in range(1, 8):
        greet(leaf, lax.rem(z + k, 8) * 2 + core)
    greet(leaf, sibling)
    pl.semaphore_wait(barrier, LEAVES + 7)

    sends = []

    def send(src, dst, st, slot, leaf_to, row_to):
        pltpu.make_async_remote_copy(
            src_ref=src,
            dst_ref=dst,
            send_sem=send_sem.at[st, slot],
            recv_sem=recv_sem.at[st, slot],
            device_id=(leaf_to, row_to),
            device_id_type=MESH,
        ).start()

    def wait(sem, st, slot, ref):
        pltpu.make_async_copy(ref, ref, sem.at[st, slot]).wait()

    def receive(st, slot, ref):
        wait(recv_sem, st, slot, ref)
        sends.append((st, slot, ref))

    def members(level):
        span = group_size(level)
        base = leaf // span * span
        return span, base, leaf - base

    def row_mask(level, first, count):
        rows = first + lax.broadcasted_iota(jnp.int32, (count, 1), 0)
        return (rows < widths[level, 0]).astype(F32)

    def cols(st):
        return pl.ds(st * PART, PART)

    def prepare_diag(s):
        if s == 0:
            diag_load.wait()
        masked = (dm[s].astype(F32) * row_mask(s, 0, WIDTH)).astype(BF16)
        dm[s] = masked
        dm_t[s] = masked.T.reshape(8, 2, ROWS, WIDTH)
        twice[s] = dot(dm_t[s, z, core], masked).astype(BF16)

    def load_blocks(t):
        for s in range(t):
            loads[s, t].wait()
        span = group_size(t)

        def scale(i, carry):
            s, p = i // span, lax.rem(i, span)
            first = OFFSETS[0, t]
            for later in range(1, t):
                first = jnp.where(s == later, OFFSETS[later, t], first)
            w = structure[0, first + p].astype(F32)
            blocks[t][s, p] = (blocks[t][s, p].astype(F32) * w).astype(BF16)
            return carry

        lax.fori_loop(0, t * span, scale, 0)

    def prepare_fold(t):
        load_blocks(t)
        span = group_size(t)

        def step(s, carry):
            flat = blocks[t][s].reshape(span * ROWS, WIDTH)
            for c in range(2):
                fold[t][s, c] = dot_nt(flat, dm_t[s, :, c].reshape(256, WIDTH)).astype(BF16)
            return carry

        lax.fori_loop(0, t, step, 0)

    def prepare_fold_t(t):
        span = group_size(t)

        def step(s, carry):
            flat = blocks[t][s].reshape(span * ROWS, WIDTH)
            for c in range(2):
                product = dot_nt(dm_t[s, :, c].reshape(256, WIDTH), flat)
                fold_t[t][s, c] = product.astype(BF16)
            return carry

        lax.fori_loop(0, t, step, 0)

    def half(st, level, c):
        return resid[st, level, :, c].reshape(256, PART)

    def prepare_pre(st, t):
        total = None
        for s in range(t - 1):
            for c in range(2):
                term = dot(fold[t][s, c], half(st, s, c))
                total = term if total is None else total + term
        if total is not None:
            pre[t][st] = total

    def outputs(st, level):
        full = resid[st, level].reshape(WIDTH, PART)
        fwd[level, 0, :, cols(st)] = dot(dm[level, own], full).astype(BF16)
        head[st, level] = dot(twice[level], full)

    def prepare_pulled(st, s):
        for c in range(2):
            total = None
            for t in range(s + 2, LEVELS):
                k = group_size(t) * ROWS
                term = dot(fold_t[t][s, c], gathered[t][st].reshape(k, PART))
                total = term if total is None else total + term
            if total is not None:
                pulled_pre[st, s, c] = total

    def send_gathered(st, level, block):
        span, base, me = members(level)
        gathered[level][st, me] = block
        for k in range(1, span):
            send(
                gathered[level].at[st, me],
                gathered[level].at[st, me],
                st,
                B_LEAF + level,
                base + lax.rem(me + k, span),
                row,
            )

    def stream(st):
        for level in range(LEVELS):
            value = rhs[level, 0, :, cols(st)].astype(F32)
            if level > 0:
                span, base, me = members(level)
                yield "leaf", level
                receive(st, LEAF + level, part_in[level].at[st, pl.ds(0, span - 1)])
                update = jnp.sum(part_in[level][st].astype(F32), axis=0)
                value = value - update
            resid[st, level, z, core] = (value * row_mask(level, row * ROWS, ROWS)).astype(BF16)
            for k in (4, 3, 5, 2, 6, 1, 7):
                send(
                    resid.at[st, level, z, core],
                    resid.at[st, level, z, core],
                    st,
                    ROW_Z + level,
                    leaf,
                    lax.rem(z + k, 8) * 2 + core,
                )
            yield "row_z", level
            receive(st, ROW_Z + level, resid.at[st, level, pl.ds(0, 7), 0])
            send(
                resid.at[st, level, :, core],
                resid.at[st, level, :, core],
                st,
                ROW_SIB + level,
                leaf,
                sibling,
            )
            target = level + 1
            if target < LEVELS:
                total = dot(fold[target][level, core], half(st, level, core))
                if target > 1:
                    total = total + pre[target][st]
                pre[target][st] = total
            yield "row_sib", level
            receive(st, ROW_SIB + level, resid.at[st, level, :, 0])
            if target < LEVELS:
                span, base, me = members(target)
                total = pre[target][st] + dot(
                    fold[target][level, other], half(st, level, other)
                )
                part_out[target][st] = total.astype(BF16).reshape(span, ROWS, PART)
                for k in range(1, span):
                    to = lax.rem(me + k, span)
                    send(
                        part_out[target].at[st, to],
                        part_in[target].at[st, me],
                        st,
                        LEAF + target,
                        base + to,
                        row,
                    )
                part_in[target][st, me] = part_out[target][st, me]
        top = LEVELS - 1
        solved = dot(twice[top], resid[st, top].reshape(WIDTH, PART))
        block = (solved * row_mask(top, row * ROWS, ROWS)).astype(BF16)
        adj[top, 0, :, cols(st)] = block
        send_gathered(st, top, block)
        for level in reversed(range(top)):
            span, base, me = members(level + 1)
            yield "b_leaf", level
            receive(st, B_LEAF + level + 1, gathered[level + 1].at[st, pl.ds(0, span - 1)])

            def pulled(c):
                values = gathered[level + 1][st].reshape(span * ROWS, PART)
                total = dot(fold_t[level + 1][level, c], values)
                if level + 2 < LEVELS:
                    total = total + pulled_pre[st, level, c]
                return total

            pulled_out[st, level] = pulled(other).astype(BF16).reshape(8, ROWS, PART)
            send(
                pulled_out.at[st, level],
                pulled_sib.at[st, level],
                st,
                B_SIB + level,
                leaf,
                sibling,
            )
            pulled_pre[st, level, core] = pulled(core)
            yield "b_sib", level
            receive(st, B_SIB + level, pulled_sib.at[st, level])
            pair = pulled_pre[st, level, core].reshape(8, ROWS, PART) + pulled_sib[
                st, level
            ].astype(F32)
            pair_out[st, level] = pair.astype(BF16)
            for k in (4, 3, 5, 2, 6, 1, 7):
                to = lax.rem(z + k, 8)
                send(
                    pair_out.at[st, level, to],
                    pair_in.at[st, level, z],
                    st,
                    B_Z + level,
                    leaf,
                    to * 2 + core,
                )
            pair_in[st, level, z] = pair_out[st, level, z]
            yield "b_z", level
            receive(st, B_Z + level, pair_in.at[st, level, pl.ds(0, 7)])
            total = jnp.sum(pair_in[st, level].astype(F32), axis=0)
            block = ((head[st, level] - total) * row_mask(level, row * ROWS, ROWS)).astype(BF16)
            adj[level, 0, :, cols(st)] = block
            if level > 0:
                send_gathered(st, level, block)

    def shared_work(kind, level):
        if kind == "row_z":
            if level == 0:
                prepare_diag(0)
                prepare_fold(1)
            elif level < LEVELS - 1:
                prepare_fold(level + 1)
            else:
                prepare_fold_t(LEVELS - 2)
        elif kind == "leaf":
            prepare_diag(level)
            if level == LEVELS - 1:
                prepare_fold_t(LEVELS - 1)
            elif level > 1:
                prepare_fold_t(level - 1)

    def stream_work(st, kind, level):
        if kind == "row_z":
            if 0 < level < LEVELS - 1:
                prepare_pre(st, level + 1)
        elif kind == "leaf":
            outputs(st, level - 1)
        elif kind == "b_leaf" and level == LEVELS - 2:
            outputs(st, LEVELS - 1)
        elif kind == "b_z" and level > 0:
            prepare_pulled(st, level - 1)

    running = [(st, stream(st)) for st in range(STREAMS)]
    while running:
        for st, steps in list(running):
            step = next(steps, None)
            if step is None:
                running.remove((st, steps))
                continue
            if st == 0:
                shared_work(*step)
            stream_work(st, *step)
    for st, slot, ref in sends:
        wait(send_sem, st, slot, ref)


def scratch_shapes():
    vmem = pltpu.VMEM
    shapes = []
    shapes += [vmem((t, group_size(t), ROWS, WIDTH), BF16) for t in TARGETS]
    shapes += [vmem((t, 2, group_size(t) * ROWS, 256), BF16) for t in TARGETS]
    shapes += [vmem((t, 2, 256, group_size(t) * ROWS), BF16) for t in TARGETS]
    shapes += [
        vmem((LEVELS, WIDTH, WIDTH), BF16),
        vmem((LEVELS, 8, 2, ROWS, WIDTH), BF16),
        vmem((LEVELS, ROWS, WIDTH), BF16),
    ]
    shapes += [vmem((STREAMS, group_size(t) * ROWS, PART), F32) for t in TARGETS]
    shapes += [vmem((STREAMS, group_size(t), ROWS, PART), BF16) for t in TARGETS]
    shapes += [vmem((STREAMS, group_size(t), ROWS, PART), BF16) for t in TARGETS]
    shapes += [vmem((STREAMS, LEVELS, 8, 2, ROWS, PART), BF16)]
    shapes += [vmem((STREAMS, group_size(t), ROWS, PART), BF16) for t in TARGETS]
    shapes += [vmem((STREAMS, LEVELS - 1, 2, 256, PART), F32)]
    shapes += [vmem((STREAMS, LEVELS - 1, 8, ROWS, PART), BF16) for _ in range(4)]
    shapes += [vmem((STREAMS, LEVELS, ROWS, PART), F32)]
    shapes += [
        pltpu.SemaphoreType.DMA((STREAMS, SLOTS)),
        pltpu.SemaphoreType.DMA((STREAMS, SLOTS)),
        pltpu.SemaphoreType.DMA((16,)),
    ]
    return shapes


def shards(rhs, diag_inverse, factor, widths, structure):
    out = jax.ShapeDtypeStruct((LEVELS, 1, ROWS, COLUMNS), BF16)
    return pl.pallas_call(
        kernel,
        out_shape=(out, out),
        in_specs=[
            pl.BlockSpec(memory_space=pltpu.VMEM),
            pl.BlockSpec(memory_space=pl.ANY),
            pl.BlockSpec(memory_space=pl.ANY),
            pl.BlockSpec(memory_space=pltpu.SMEM),
            pl.BlockSpec(memory_space=pltpu.SMEM),
        ],
        out_specs=(
            pl.BlockSpec(memory_space=pltpu.VMEM),
            pl.BlockSpec(memory_space=pltpu.VMEM),
        ),
        scratch_shapes=scratch_shapes(),
        compiler_params=pltpu.CompilerParams(
            collective_id=0, has_side_effects=True, vmem_limit_bytes=52 * 2**20
        ),
    )(rhs, diag_inverse, factor, widths, structure)


def solution(mesh):
    placed = (
        P(None, "leaf", "row", None),
        P("leaf", None, None, None),
        P("leaf", None, "row", None),
        P(None, "leaf"),
        P("leaf", None),
    )
    return jax.shard_map(
        shards,
        mesh=mesh,
        in_specs=placed,
        out_specs=(P(None, "leaf", "row", None), P(None, "leaf", "row", None)),
        check_vma=False,
    )
```

```python
import jax
import jax.numpy as jnp
from jax import lax
from jax.experimental import pallas as pl
from jax.experimental.pallas import tpu as pltpu
from jax.sharding import PartitionSpec as P

MESH = pl.DeviceIdType.MESH
F32 = jnp.float32
BF16 = jnp.bfloat16
LEVELS = 6
LEAVES = 16
CHIPS = 8
ROWS = 32
PAIR = 2 * ROWS
WIDTH = 512
COLUMNS = 256
PART = COLUMNS // 2
TARGETS = tuple(range(1, LEVELS))
TOP = LEVELS - 1
FAR_FIRST = (4, 3, 5, 2, 6, 1, 7)


def group_size(level):
    return min(2**level, LEAVES)


def block_offsets():
    table, cursor = {}, 0
    for source in range(LEVELS):
        for target in range(source + 1, LEVELS):
            table[source, target] = cursor
            cursor += group_size(target)
    return table


OFFSETS = block_offsets()


def dot(a, b):
    return jnp.dot(a, b, preferred_element_type=F32)


def dot_nt(a, b):
    return lax.dot_general(a, b, (((1,), (1,)), ((), ())), preferred_element_type=F32)


ROW_Z, LEAF, B_LEAF, B_Z, FOLD, FOLD_T = (i * LEVELS for i in range(6))
RHS_X, FWD_X, HEAD_X = (6 * LEVELS + i for i in range(3))
SLOTS = 6 * LEVELS + 3


def kernel(rhs_hbm, diag, factor, widths_hbm, structure_hbm, fwd, adj, *scratch):
    scratch = list(scratch)

    def take(n):
        out = scratch[:n]
        del scratch[:n]
        return out

    per_target = lambda: dict(zip(TARGETS, take(len(TARGETS))))
    blocks, fold, fold_t = per_target(), per_target(), per_target()
    dm, dm_t, twice = take(3)
    pre, part_out, part_in = per_target(), per_target(), per_target()
    (resid,) = take(1)
    gathered = per_target()
    pulled_pre, pair_out, pair_in, head = take(4)
    rhs, rhs_out, rhs_in, fwd_out, fwd_in, head_in, first_out = take(7)
    widths, structure = take(2)
    send_sem, recv_sem, load_sem = take(3)

    leaf = lax.axis_index("leaf")
    row = lax.axis_index("row")
    z, core = row // 2, lax.rem(row, 2)
    other = 1 - core
    sibling = z * 2 + other
    quarter = z // 2

    loads = {}

    def load(name, src, dst):
        loads[name] = pltpu.make_async_copy(src, dst, load_sem.at[len(loads)])
        loads[name].start()

    load("widths", widths_hbm, widths)
    load("rhs", rhs_hbm.at[:, 0], rhs)
    load("structure", structure_hbm, structure)
    load("diag", diag.at[0], dm)
    for t in TARGETS:
        for s in range(t):
            load((s, t), factor.at[0, pl.ds(OFFSETS[s, t], group_size(t))], blocks[t].at[s])

    barrier = pltpu.get_barrier_semaphore()

    def greet(leaf_to, row_to):
        pl.semaphore_signal(barrier, inc=1, device_id=(leaf_to, row_to), device_id_type=MESH)

    for k in FAR_FIRST:
        for c in range(2):
            greet(leaf, lax.rem(z + k, CHIPS) * 2 + c)
    greet(leaf, sibling)
    for k in range(1, LEAVES):
        greet(lax.rem(leaf + k, LEAVES), row)

    sends = []

    def send(src, dst, slot, leaf_to, row_to):
        pltpu.make_async_remote_copy(
            src_ref=src,
            dst_ref=dst,
            send_sem=send_sem.at[slot],
            recv_sem=recv_sem.at[slot],
            device_id=(leaf_to, row_to),
            device_id_type=MESH,
        ).start()

    def wait(sem, slot, ref):
        pltpu.make_async_copy(ref, ref, sem.at[slot]).wait()

    def receive(slot, ref):
        wait(recv_sem, slot, ref)
        sends.append((slot, ref))

    def members(level):
        span = group_size(level)
        base = leaf // span * span
        return span, base, leaf - base

    def row_mask(level, first, count):
        rows = first + lax.broadcasted_iota(jnp.int32, (count, 1), 0)
        return (rows < widths[level]).astype(F32)

    def pair_mask(level):
        return row_mask(level, z * PAIR, PAIR)

    def prepare_diag(s):
        masked = (dm[s].astype(F32) * row_mask(s, 0, WIDTH)).astype(BF16)
        dm[s] = masked
        dm_t[s] = masked.T.reshape(CHIPS, PAIR, WIDTH)
        twice[s] = dot(dm_t[s, z], masked).astype(BF16)

    def load_blocks(t):
        for s in range(t):
            loads[s, t].wait()
        span = group_size(t)

        def scale(i, carry):
            s, p = i // span, lax.rem(i, span)
            first = OFFSETS[0, t]
            for later in range(1, t):
                first = jnp.where(s == later, OFFSETS[later, t], first)
            w = structure[0, first + p].astype(F32)
            blocks[t][s, p] = (blocks[t][s, p].astype(F32) * w).astype(BF16)
            return carry

        lax.fori_loop(0, t * span, scale, 0)

    def prepare_fold(t):
        load_blocks(t)
        span = group_size(t)

        def step(s, carry):
            flat = blocks[t][s].reshape(span * ROWS, WIDTH)
            for c in range(2):
                cols = pl.ds(c * 256, 256)
                part = dot_nt(flat, dm_t[s, pl.ds(c * 4, 4)].reshape(256, WIDTH))
                fold[t][s, :, core, :, cols] = part.astype(BF16).reshape(span, ROWS, 256)
            return carry

        lax.fori_loop(0, t, step, 0)
        mine = fold[t].at[:, :, core]
        send(mine, mine, FOLD + t, leaf, sibling)

    def prepare_fold_t(t):
        span = group_size(t)

        def step(s, carry):
            flat = blocks[t][s].reshape(span * ROWS, WIDTH)
            for c in range(2):
                part = dot_nt(dm_t[s, pl.ds(c * 4, 4)].reshape(256, WIDTH), flat)
                fold_t[t][s, core, pl.ds(c * 2, 2)] = part.astype(BF16).reshape(
                    2, 128, span * ROWS
                )
            return carry

        lax.fori_loop(0, t, step, 0)
        mine = fold_t[t].at[:, core]
        send(mine, mine, FOLD_T + t, leaf, sibling)

    def full(level):
        return resid[level].reshape(WIDTH, PART)

    def prepare_pre(t):
        receive(FOLD + t, fold[t].at[:, :, 0])
        height = group_size(t) * PAIR
        if t > 1:
            total = None
            for s in range(t - 1):
                term = dot(fold[t][s].reshape(height, WIDTH), full(s))
                total = term if total is None else total + term
            pre[t][...] = total.reshape(group_size(t), PAIR, PART)

    def outputs(level):
        rows = pl.ds(pl.multiple_of(z * PAIR, PAIR), PAIR)
        fwd_out[level] = dot(dm[level, rows], full(level)).astype(BF16).reshape(2, ROWS, PART)
        head[level] = dot(twice[level], full(level)).reshape(2, ROWS, PART)

    def prepare_pulled(s):
        total = None
        for t in range(s + 2, LEVELS):
            k = group_size(t) * ROWS
            for b in range(2):
                term = dot(
                    fold_t[t][s, b].reshape(WIDTH, k), gathered[t][b].reshape(k, PART)
                )
                total = term if total is None else total + term
        pulled_pre[s] = total.reshape(4, 128, PART)

    def send_gathered(level, block):
        span, base, me = members(level)
        gathered[level][:, me] = block
        mine = gathered[level].at[:, me]
        for to in neighbours(span, me):
            send(mine, mine, B_LEAF + level, base + to, row)

    def grid_of(span):
        deep = min(span, 4)
        return span // deep, deep

    ORDER = {1: (0,), 2: (1, 0), 4: (2, 1, 3, 0)}

    def neighbours(span, me):
        wide, deep = grid_of(span)
        for dx in ORDER[wide]:
            for dy in ORDER[deep]:
                if dx or dy:
                    x = lax.rem(me // deep + dx, wide)
                    yield x * deep + lax.rem(lax.rem(me, deep) + dy, deep)

    loads["widths"].wait()
    loads["rhs"].wait()
    first = (rhs[0].astype(F32) * row_mask(0, row * ROWS, ROWS)).astype(BF16)
    for c in range(2):
        first_out[c] = first[:, c * PART : (c + 1) * PART]
        rhs_out[c] = rhs[:, :, c * PART : (c + 1) * PART]
    mine = pl.ds(pl.multiple_of(core * ROWS, ROWS), ROWS)
    resid[0, z, mine] = first_out[core]
    pl.semaphore_wait(barrier, LEAVES + 14)
    for k in FAR_FIRST:
        for c in range(2):
            send(
                first_out.at[c],
                resid.at[0, z, mine],
                ROW_Z,
                leaf,
                lax.rem(z + k, CHIPS) * 2 + c,
            )
    send(first_out.at[other], resid.at[0, z, mine], ROW_Z, leaf, sibling)
    send(rhs_out.at[other], rhs_in.at[core], RHS_X, leaf, sibling)
    rhs_in[core] = rhs_out[core]

    for level in range(LEVELS):
        if level > 0:
            span, base, me = members(level)
            receive(LEAF + level, part_in[level].at[pl.ds(0, span - 1)])
            update = jnp.sum(part_in[level][...].astype(F32), axis=0)
            value = rhs_in[:, level].reshape(PAIR, PART).astype(F32) - update
            resid[level, z] = (value * pair_mask(level)).astype(BF16)
            for k in FAR_FIRST:
                send(
                    resid.at[level, z],
                    resid.at[level, z],
                    ROW_Z + level,
                    leaf,
                    lax.rem(z + k, CHIPS) * 2 + core,
                )
        if level == 0:
            loads["diag"].wait()
            loads["structure"].wait()
            prepare_diag(0)
            prepare_fold(1)
            prepare_diag(1)
            prepare_fold(2)
        elif level == 1:
            prepare_diag(3)
            prepare_fold(4)
        elif level == 2:
            prepare_fold(5)
        elif level == 3:
            prepare_fold_t(4)
        elif level == 4:
            prepare_fold_t(3)
        else:
            outputs(4)
            head_mine = head.at[0, other]
            send(head_mine, head_in, HEAD_X, leaf, sibling)
        if level < TOP:
            prepare_pre(level + 1)
        if level == 0:
            receive(ROW_Z, resid.at[pl.ds(0, 5), pl.ds(0, 3), pl.ds(0, ROWS)])
        else:
            receive(ROW_Z + level, resid.at[level, pl.ds(0, 7)])
        if level == TOP:
            break
        target = level + 1
        span, base, me = members(target)
        wide, deep = grid_of(span)
        values = full(level)
        for dx in ORDER[wide]:
            x = lax.rem(me // deep + dx, wide)
            group = pl.ds(x * deep, deep)
            total = dot(fold[target][level, group].reshape(deep * PAIR, WIDTH), values)
            total = total.reshape(deep, PAIR, PART)
            if target > 1:
                total = total + pre[target][group]
            part_out[target][group] = total.astype(BF16)
            for dy in ORDER[deep]:
                to = x * deep + lax.rem(lax.rem(me, deep) + dy, deep)
                if dx or dy:
                    send(
                        part_out[target].at[to],
                        part_in[target].at[me],
                        LEAF + target,
                        base + to,
                        row,
                    )
        part_in[target][me] = part_out[target][me]
        if level == 0:
            prepare_diag(2)
            prepare_fold(3)
            receive(RHS_X, rhs_in.at[0])
        elif level == 1:
            prepare_diag(4)
            prepare_fold_t(1)
        elif level == 2:
            prepare_diag(5)
            outputs(0)
            outputs(1)
        elif level == 3:
            outputs(2)
            prepare_fold_t(5)
        else:
            outputs(3)
            prepare_fold_t(2)
    solved = dot(twice[TOP], full(TOP))
    block = (solved * pair_mask(TOP)).astype(BF16).reshape(2, ROWS, PART)
    adj_out = fwd_out.at[pl.ds(LEVELS, LEVELS)]
    adj_out[0] = jnp.zeros((2, ROWS, PART), BF16)
    adj_out[TOP] = block
    send_gathered(TOP, block)
    for level in reversed(range(TOP)):
        upper = level + 1
        span, base, me = members(upper)
        if level == TOP - 1:
            outputs(TOP)
            for t in reversed(TARGETS):
                receive(FOLD_T + t, fold_t[t].at[:, 0])
        receive(B_LEAF + upper, gathered[upper].at[:, pl.ds(0, span - 1)])
        values = [gathered[upper][b].reshape(span * ROWS, PART) for b in range(2)]
        for dq in (2, 0):
            quarters = [lax.rem(quarter + dq + i, 4) for i in range(2)]
            total = None
            for b in range(2):
                side = jnp.concatenate([fold_t[upper][level, b, q] for q in quarters], axis=0)
                term = dot(side, values[b])
                total = term if total is None else total + term
            for i, q in enumerate(quarters):
                piece = total[i * 128 : (i + 1) * 128]
                if upper < TOP:
                    piece = piece + pulled_pre[level, q]
                pair_out[level, pl.ds(q * 2, 2)] = piece.astype(BF16).reshape(2, 2, ROWS, PART)
            for k in (4, 5, 6) if dq else (3, 2, 1, 7):
                to = lax.rem(z + k, CHIPS)
                if level > 0:
                    send(
                        pair_out.at[level, to],
                        pair_in.at[level, z],
                        B_Z + level,
                        leaf,
                        to * 2 + core,
                    )
                else:
                    for b in range(2):
                        send(
                            pair_out.at[0, to, b],
                            pair_in.at[0, z, core],
                            B_Z,
                            leaf,
                            to * 2 + b,
                        )
        if level > 0:
            pair_in[level, z] = pair_out[level, z]
        else:
            send(pair_out.at[0, z, other], pair_in.at[0, z, core], B_Z, leaf, sibling)
            pair_in[0, z, core] = pair_out[0, z, core]
        if level > 0:
            prepare_pulled(level - 1)
            receive(B_Z + level, pair_in.at[level, pl.ds(0, 7)])
            pulled = jnp.sum(pair_in[level].astype(F32), axis=0)
            mask = pair_mask(level).reshape(2, ROWS, 1)
            block = ((head[level] - pulled) * mask).astype(BF16)
            adj_out[level] = block
            send_gathered(level, block)
            if level == 1:
                send(fwd_out.at[:, other], fwd_in, FWD_X, leaf, sibling)
                receive(HEAD_X, head_in)
        else:
            receive(FWD_X, fwd_in)
            for out, part in ((fwd, 0), (adj, LEVELS)):
                for lv in range(LEVELS):
                    if part and not lv:
                        continue
                    for c in range(2):
                        block = jnp.where(core == c, fwd_out[part + lv, core], fwd_in[part + lv])
                        out[lv, 0, :, pl.ds(c * PART, PART)] = block
            receive(B_Z, pair_in.at[pl.ds(0, 5), pl.ds(0, 3), 0])
            pulled = jnp.sum(pair_in[0].astype(F32), axis=0)
            mask = row_mask(0, row * ROWS, ROWS)
            for c in range(2):
                ahead = jnp.where(core == c, head[0, core], head_in[...])
                adj[0, 0, :, pl.ds(c * PART, PART)] = ((ahead - pulled[c]) * mask).astype(BF16)
    for slot, ref in sends:
        wait(send_sem, slot, ref)


def scratch_shapes():
    vmem = pltpu.VMEM
    shapes = []
    shapes += [vmem((t, group_size(t), ROWS, WIDTH), BF16) for t in TARGETS]
    shapes += [vmem((t, group_size(t), 2, ROWS, WIDTH), BF16) for t in TARGETS]
    shapes += [vmem((t, 2, 4, 128, group_size(t) * ROWS), BF16) for t in TARGETS]
    shapes += [
        vmem((LEVELS, WIDTH, WIDTH), BF16),
        vmem((LEVELS, CHIPS, PAIR, WIDTH), BF16),
        vmem((LEVELS, PAIR, WIDTH), BF16),
    ]
    shapes += [vmem((group_size(t), PAIR, PART), F32) for t in TARGETS]
    shapes += [vmem((group_size(t), PAIR, PART), BF16) for t in TARGETS]
    shapes += [vmem((group_size(t), PAIR, PART), BF16) for t in TARGETS]
    shapes += [vmem((LEVELS, CHIPS, PAIR, PART), BF16)]
    shapes += [vmem((2, group_size(t), ROWS, PART), BF16) for t in TARGETS]
    shapes += [
        vmem((TOP, 4, 128, PART), F32),
        vmem((TOP, CHIPS, 2, ROWS, PART), BF16),
        vmem((TOP, CHIPS, 2, ROWS, PART), BF16),
        vmem((LEVELS, 2, ROWS, PART), F32),
        vmem((LEVELS, ROWS, COLUMNS), BF16),
        vmem((2, LEVELS, ROWS, PART), BF16),
        vmem((2, LEVELS, ROWS, PART), BF16),
        vmem((2 * LEVELS, 2, ROWS, PART), BF16),
        vmem((2 * LEVELS, ROWS, PART), BF16),
        vmem((ROWS, PART), F32),
        vmem((2, ROWS, PART), BF16),
        pltpu.SMEM((LEVELS,), jnp.int32),
        pltpu.SMEM((1, 178), jnp.int32),
        pltpu.SemaphoreType.DMA((SLOTS,)),
        pltpu.SemaphoreType.DMA((SLOTS,)),
        pltpu.SemaphoreType.DMA((24,)),
    ]
    return shapes


def shards(rhs, diag_inverse, factor, widths, structure):
    out = jax.ShapeDtypeStruct((LEVELS, 1, ROWS, COLUMNS), BF16)
    return pl.pallas_call(
        kernel,
        out_shape=(out, out),
        in_specs=[pl.BlockSpec(memory_space=pltpu.HBM)] * 5,
        out_specs=[pl.BlockSpec(memory_space=pltpu.VMEM)] * 2,
        scratch_shapes=scratch_shapes(),
        compiler_params=pltpu.CompilerParams(
            collective_id=0, has_side_effects=True, vmem_limit_bytes=56 * 2**20
        ),
    )(rhs, diag_inverse, factor, widths.reshape(LEVELS), structure)


def solution(mesh):
    placed = (
        P(None, "leaf", "row", None),
        P("leaf", None, None, None),
        P("leaf", None, "row", None),
        P(None, "leaf"),
        P("leaf", None),
    )
    return jax.shard_map(
        shards,
        mesh=mesh,
        in_specs=placed,
        out_specs=(P(None, "leaf", "row", None), P(None, "leaf", "row", None)),
        check_vma=False,
    )
```

```python
import jax
import jax.numpy as jnp
from jax import lax
from jax.experimental import pallas as pl
from jax.experimental.pallas import tpu as pltpu
from jax.sharding import PartitionSpec as P

MESH = pl.DeviceIdType.MESH
F32 = jnp.float32
BF16 = jnp.bfloat16
LEVELS = 6
LEAVES = 16
CHIPS = 8
ROWS = 32
PAIR = 2 * ROWS
WIDTH = 512
COLUMNS = 256
PART = COLUMNS // 2
TARGETS = tuple(range(1, LEVELS))
TOP = LEVELS - 1
Z_ORDER = (0, 1, 7, 2, 6, 3, 5, 4)
Z_SLOT = {d: i for i, d in enumerate(Z_ORDER)}
FAR_FIRST = Z_ORDER[:0:-1]


def group_size(level):
    return min(2**level, LEAVES)


def block_offsets():
    table, cursor = {}, 0
    for source in range(LEVELS):
        for target in range(source + 1, LEVELS):
            table[source, target] = cursor
            cursor += group_size(target)
    return table


OFFSETS = block_offsets()


def dot(a, b):
    return jnp.dot(a, b, preferred_element_type=F32)


def dot_nt(a, b):
    return lax.dot_general(a, b, (((1,), (1,)), ((), ())), preferred_element_type=F32)


ROW_Z, LEAF, B_LEAF, B_Z = (i * 2 * LEVELS for i in range(4))
FOLD, FOLD_T = 8 * LEVELS, 9 * LEVELS
RHS_X, FWD_X, HEAD_X = (10 * LEVELS + i for i in range(3))
SLOTS = 10 * LEVELS + 3


def ring(d, n):
    return min(d, n - d) if n > 2 else d


def extent(span):
    deep = min(span, 4)
    return span // deep, deep


def leaf_order(span):
    wide, deep = extent(span)
    steps = [(dx, dy) for dx in range(wide) for dy in range(deep)]
    return sorted(steps, key=lambda d: ring(d[0], wide) + ring(d[1], deep))


def leaf_back(span, step):
    wide, deep = extent(span)
    return leaf_order(span).index((-step[0] % wide, -step[1] % deep))


def kernel(rhs_hbm, diag, factor, widths_hbm, structure_hbm, fwd, adj, *scratch):
    scratch = list(scratch)

    def take(n):
        out = scratch[:n]
        del scratch[:n]
        return out

    per_target = lambda: dict(zip(TARGETS, take(len(TARGETS))))
    blocks, sorted_blocks, fold, fold_t = per_target(), per_target(), per_target(), per_target()
    dm, dm_t, own_rows, twice, turned = take(5)
    pre, part_out, part_in = per_target(), per_target(), per_target()
    (resid,) = take(1)
    gathered = per_target()
    pulled_pre, pair_out, pair_in, head = take(4)
    rhs, rhs_out, rhs_in, fwd_out, fwd_in, head_in, first_out, whole = take(8)
    widths, structure = take(2)
    send_sem, recv_sem, load_sem, out_sem = take(4)

    leaf = lax.axis_index("leaf")
    row = lax.axis_index("row")
    z, core = row // 2, lax.rem(row, 2)
    other = 1 - core
    sibling = z * 2 + other

    barrier = pltpu.get_barrier_semaphore()

    def greet(leaf_to, row_to):
        pl.semaphore_signal(barrier, inc=1, device_id=(leaf_to, row_to), device_id_type=MESH)

    for k in FAR_FIRST:
        for c in range(2):
            greet(leaf, lax.rem(z + k, CHIPS) * 2 + c)
    for k in range(1, LEAVES):
        greet(lax.rem(leaf + k, LEAVES), row)
    greet(leaf, sibling)

    loads = {}

    def load(name, src, dst):
        loads[name] = pltpu.make_async_copy(src, dst, load_sem.at[len(loads)])
        loads[name].start()

    load("widths", widths_hbm, widths)
    load("rhs", rhs_hbm.at[:, 0], rhs)
    load("structure", structure_hbm, structure)
    load("diag", diag.at[0], dm)
    for t in TARGETS:
        for s in range(t):
            load((s, t), factor.at[0, pl.ds(OFFSETS[s, t], group_size(t))], blocks[t].at[s])

    sends = []

    def send(src, dst, slot, leaf_to, row_to):
        pltpu.make_async_remote_copy(
            src_ref=src,
            dst_ref=dst,
            send_sem=send_sem.at[slot],
            recv_sem=recv_sem.at[slot],
            device_id=(leaf_to, row_to),
            device_id_type=MESH,
        ).start()

    def wait(sem, slot, ref):
        pltpu.make_async_copy(ref, ref, sem.at[slot]).wait()

    def receive(slot, ref):
        wait(recv_sem, slot, ref)
        sends.append((slot, ref))

    def member(span, step):
        wide, deep = extent(span)
        me = lax.rem(leaf, span)
        x = lax.rem(me // deep + step[0], wide)
        return x * deep + lax.rem(lax.rem(me, deep) + step[1], deep)

    def leaf_of(span, step):
        return leaf // span * span + member(span, step)

    def row_mask(level, first, count):
        rows = first + lax.broadcasted_iota(jnp.int32, (count, 1), 0)
        return (rows < widths[level]).astype(F32)

    def pair_mask(level):
        return row_mask(level, z * PAIR, PAIR)

    def prepare_diag(s):
        masked = (dm[s].astype(F32) * row_mask(s, 0, WIDTH)).astype(BF16)
        turned[...] = masked.T.reshape(CHIPS, PAIR, WIDTH)
        for i, d in enumerate(Z_ORDER):
            dm_t[s, i] = turned[lax.rem(z + d, CHIPS)]
        everything = dm_t[s].reshape(WIDTH, WIDTH)
        twice[s] = dot_nt(dm_t[s, 0], everything).astype(BF16)
        wanted = z * PAIR + lax.broadcasted_iota(jnp.int32, (PAIR, WIDTH), 0)
        at = lax.broadcasted_iota(jnp.int32, (PAIR, WIDTH), 1)
        chosen = (at == wanted).astype(F32).astype(BF16)
        own_rows[s] = dot_nt(chosen, everything).astype(BF16)

    def sort_blocks(t):
        for s in range(t):
            loads[s, t].wait()
        span = group_size(t)

        def scale(s, carry):
            first = OFFSETS[0, t]
            for later in range(1, t):
                first = jnp.where(s == later, OFFSETS[later, t], first)
            for i, step in enumerate(leaf_order(span)):
                p = member(span, step)
                w = structure[0, first + p].astype(F32)
                sorted_blocks[t][s, i] = (blocks[t][s, p].astype(F32) * w).astype(BF16)
            return carry

        lax.fori_loop(0, t, scale, 0)

    def prepare_fold(t):
        sort_blocks(t)
        span = group_size(t)

        def step(s, carry):
            flat = sorted_blocks[t][s].reshape(span * ROWS, WIDTH)
            for k in range(2):
                part = dot_nt(flat, dm_t[s, pl.ds(k * 4, 4)].reshape(256, WIDTH)).astype(BF16)
                fold[t][s, :, core, :, k * 256 : (k + 1) * 256] = part.reshape(span, ROWS, 256)
            return carry

        lax.fori_loop(0, t, step, 0)
        mine = fold[t].at[:, :, core]
        send(mine, mine, FOLD + t, leaf, sibling)

    def prepare_fold_t(t):
        height = group_size(t) * ROWS

        def step(s, carry):
            flat = sorted_blocks[t][s].reshape(height, WIDTH)
            for m in range(2):
                part = dot_nt(dm_t[s, pl.ds(m * 4, 4)].reshape(256, WIDTH), flat)
                fold_t[t][s, core, m] = part.astype(BF16)
            return carry

        lax.fori_loop(0, t, step, 0)
        mine = fold_t[t].at[:, core]
        send(mine, mine, FOLD_T + t, leaf, sibling)

    def prepare_third():
        prepare_diag(2)
        prepare_fold(3)

    def full(level):
        return resid[level].reshape(WIDTH, PART)

    def prepare_pre(t):
        receive(FOLD + t, fold[t].at[:, :, 0])
        height = group_size(t) * PAIR
        total = None
        for s in range(t - 1):
            term = dot(fold[t][s].reshape(height, WIDTH), full(s))
            total = term if total is None else total + term
        if total is not None:
            pre[t][...] = total

    def outputs(level):
        fwd_out[level] = dot(own_rows[level], full(level)).astype(BF16).reshape(2, ROWS, PART)
        head[level] = dot(twice[level], full(level)).reshape(2, ROWS, PART)

    def prepare_pulled(s):
        for m in range(2):
            total = None
            for t in range(s + 2, LEVELS):
                for b in range(2):
                    values = gathered[t][b].reshape(group_size(t) * ROWS, PART)
                    term = dot(fold_t[t][s, b, m], values)
                    total = term if total is None else total + term
            pulled_pre[s, m] = total

    def send_gathered(level, block):
        span = group_size(level)
        gathered[level][:, 0] = block
        for step in reversed(leaf_order(span)[1:]):
            there = leaf_back(span, step)
            send(
                gathered[level].at[:, 0],
                gathered[level].at[:, there],
                B_LEAF + 2 * level + (2 * there >= span),
                leaf_of(span, step),
                row,
            )

    loads["widths"].wait()
    loads["rhs"].wait()
    first = (rhs[0].astype(F32) * row_mask(0, row * ROWS, ROWS)).astype(BF16)
    for c in range(2):
        first_out[c] = first[:, c * PART : (c + 1) * PART]
        rhs_out[c] = rhs[:, :, c * PART : (c + 1) * PART]
    mine = pl.ds(pl.multiple_of(core * ROWS, ROWS), ROWS)
    resid[0, 0, mine] = first_out[core]
    pl.semaphore_wait(barrier, LEAVES + 14)
    for d in FAR_FIRST:
        there = resid.at[0, Z_SLOT[-d % CHIPS], mine]
        for c in range(2):
            to = lax.rem(z + d, CHIPS) * 2 + c
            send(first_out.at[c], there, ROW_Z + (Z_SLOT[-d % CHIPS] > 3), leaf, to)
    send(first_out.at[other], resid.at[0, 0, mine], ROW_Z, leaf, sibling)
    send(rhs_out.at[other], rhs_in.at[core], RHS_X, leaf, sibling)
    rhs_in[core] = rhs_out[core]

    for level in range(LEVELS):
        if level > 0:
            span = group_size(level)
            near = span // 2
            value = rhs_in[:, level].reshape(PAIR, PART).astype(F32)
            if near > 1:
                receive(LEAF + 2 * level, part_in[level].at[pl.ds(0, near - 1)])
            value = value - jnp.sum(part_in[level][:near].astype(F32), axis=0)
            receive(LEAF + 2 * level + 1, part_in[level].at[pl.ds(0, near)])
            value = value - jnp.sum(part_in[level][near:].astype(F32), axis=0)
            resid[level, 0] = (value * pair_mask(level)).astype(BF16)
            for d in FAR_FIRST:
                there = Z_SLOT[-d % CHIPS]
                send(
                    resid.at[level, 0],
                    resid.at[level, there],
                    ROW_Z + 2 * level + (there > 3),
                    leaf,
                    lax.rem(z + d, CHIPS) * 2 + core,
                )
        if level == 0:
            loads["diag"].wait()
            loads["structure"].wait()
            prepare_diag(0)
            prepare_fold(1)
            prepare_diag(1)
            prepare_fold(2)
        elif level == 1:
            prepare_diag(3)
            prepare_fold(4)
        elif level == 2:
            prepare_fold(5)
        elif level == 3:
            prepare_fold_t(4)
        elif level == 4:
            prepare_fold_t(3)
        else:
            outputs(4)
            send(head.at[0, other], head_in, HEAD_X, leaf, sibling)
        target = level + 1
        if level < TOP:
            prepare_pre(target)
            span = group_size(target)
            near = span // 2
            height = near * PAIR
        for k in range(2):
            if level > 0:
                receive(ROW_Z + 2 * level + k, resid.at[level, pl.ds(0, 3 + k)])
            elif k:
                receive(ROW_Z + 1, resid.at[pl.ds(0, 4), pl.ds(0, 2), pl.ds(0, ROWS)])
            else:
                receive(ROW_Z, resid.at[0, pl.ds(0, 7), pl.ds(0, ROWS)])
            if level == TOP:
                continue
            if level == 0 and k:
                pl.when(core == 1)(prepare_third)
            values = resid[level, k * 4 : k * 4 + 4].reshape(256, PART)
            for m in (1, 0):
                rows = slice(m * height, (m + 1) * height)
                half = fold[target][level, m * near : (m + 1) * near]
                half = half.reshape(height, WIDTH)[:, k * 256 : (k + 1) * 256]
                total = dot(half, values)
                if target > 1 or k:
                    total = total + pre[target][rows]
                if k == 0:
                    pre[target][rows] = total
                    continue
                total = total.astype(BF16).reshape(near, PAIR, PART)
                part_out[target][m * near : (m + 1) * near] = total
                for i in reversed(range(max(m * near, 1), (m + 1) * near)):
                    step = leaf_order(span)[i]
                    there = leaf_back(span, step)
                    send(
                        part_out[target].at[i],
                        part_in[target].at[there],
                        LEAF + 2 * target + (there >= near),
                        leaf_of(span, step),
                        row,
                    )
                if m == 0:
                    part_in[target][0] = part_out[target][0]
        if level == 0:
            pl.when(core == 0)(prepare_third)
            receive(RHS_X, rhs_in.at[0])
        elif level == 1:
            prepare_diag(4)
            prepare_fold_t(1)
        elif level == 2:
            prepare_diag(5)
            outputs(0)
            outputs(1)
        elif level == 3:
            outputs(2)
            prepare_fold_t(5)
        elif level == 4:
            outputs(3)
            prepare_fold_t(2)
    solved = dot(twice[TOP], full(TOP))
    block = (solved * pair_mask(TOP)).astype(BF16).reshape(2, ROWS, PART)
    adj_out = fwd_out.at[pl.ds(LEVELS, LEVELS)]
    adj_out[0] = jnp.zeros((2, ROWS, PART), BF16)
    adj_out[TOP] = block
    send_gathered(TOP, block)
    for level in reversed(range(TOP)):
        upper = level + 1
        span = group_size(upper)
        near = span // 2
        if level == TOP - 1:
            outputs(TOP)
            for t in reversed(TARGETS):
                receive(FOLD_T + t, fold_t[t].at[:, 0])
        begun = upper < TOP
        for k in range(2):
            if k:
                receive(B_LEAF + 2 * upper + 1, gathered[upper].at[:, pl.ds(0, near)])
            elif near > 1:
                receive(B_LEAF + 2 * upper, gathered[upper].at[:, pl.ds(0, near - 1)])
            if span >= 8:
                first, count = k * near, near
            elif k:
                first, count = 0, span
            else:
                continue
            for m in (1, 0):
                total = None
                for b in range(2):
                    values = gathered[upper][b, first : first + count]
                    half = fold_t[upper][
                        level, b, m, :, first * ROWS : (first + count) * ROWS
                    ]
                    term = dot(half, values.reshape(count * ROWS, PART))
                    total = term if total is None else total + term
                if begun:
                    total = total + pulled_pre[level, m]
                if k == 0:
                    pulled_pre[level, m] = total
                    continue
                pair_out[level, m * 4 : m * 4 + 4] = total.astype(BF16).reshape(4, 2, ROWS, PART)
                for d in reversed(Z_ORDER[max(m * 4, 1) : m * 4 + 4]):
                    i, there = Z_SLOT[d], Z_SLOT[-d % CHIPS]
                    to = lax.rem(z + d, CHIPS)
                    slot = B_Z + 2 * level + (there > 3)
                    if level > 0:
                        send(
                            pair_out.at[level, i],
                            pair_in.at[level, there],
                            slot,
                            leaf,
                            to * 2 + core,
                        )
                        continue
                    for b in range(2):
                        landing = pair_in.at[0, there, core]
                        send(pair_out.at[0, i, b], landing, slot, leaf, to * 2 + b)
            begun = True
        if level > 0:
            pair_in[level, 0] = pair_out[level, 0]
            prepare_pulled(level - 1)
            value = head[level]
            receive(B_Z + 2 * level, pair_in.at[level, pl.ds(0, 3)])
            value = value - jnp.sum(pair_in[level, :4].astype(F32), axis=0)
            receive(B_Z + 2 * level + 1, pair_in.at[level, pl.ds(0, 4)])
            value = value - jnp.sum(pair_in[level, 4:].astype(F32), axis=0)
            block = (value * pair_mask(level).reshape(2, ROWS, 1)).astype(BF16)
            adj_out[level] = block
            send_gathered(level, block)
            if level == 1:
                send(fwd_out.at[:, other], fwd_in, FWD_X, leaf, sibling)
                receive(HEAD_X, head_in)
            continue
        send(pair_out.at[0, 0, other], pair_in.at[0, 0, core], B_Z, leaf, sibling)
        pair_in[0, 0, core] = pair_out[0, 0, core]
        receive(FWD_X, fwd_in)
        for i in range(2 * LEVELS):
            if i == LEVELS:
                continue
            for c in range(2):
                block = jnp.where(core == c, fwd_out[i, core], fwd_in[i])
                whole[i, :, c * PART : (c + 1) * PART] = block
        stores = [
            (whole.at[pl.ds(0, LEVELS)], fwd.at[:, 0]),
            (whole.at[pl.ds(LEVELS + 1, TOP)], adj.at[pl.ds(1, TOP), 0]),
            (whole.at[LEVELS], adj.at[0, 0]),
        ]
        stores = [pltpu.make_async_copy(*pair, out_sem.at[i]) for i, pair in enumerate(stores)]
        stores[0].start()
        stores[1].start()
        receive(B_Z, pair_in.at[0, pl.ds(0, 7), 0])
        near_sum = jnp.sum(pair_in[0, :4].astype(F32), axis=0)
        receive(B_Z + 1, pair_in.at[0, pl.ds(0, 4)])
        pulled = near_sum + jnp.sum(pair_in[0, 4:].astype(F32), axis=0)
        mask = row_mask(0, row * ROWS, ROWS)
        for c in range(2):
            ahead = jnp.where(core == c, head[0, core], head_in[...])
            block = ((ahead - pulled[c]) * mask).astype(BF16)
            whole[LEVELS, :, c * PART : (c + 1) * PART] = block
        stores[2].start()
        for slot, ref in sends:
            wait(send_sem, slot, ref)
        for store in stores:
            store.wait()


def scratch_shapes():
    vmem = pltpu.VMEM
    shapes = []
    for _ in range(2):
        shapes += [vmem((t, group_size(t), ROWS, WIDTH), BF16) for t in TARGETS]
    shapes += [vmem((t, group_size(t), 2, ROWS, WIDTH), BF16) for t in TARGETS]
    shapes += [vmem((t, 2, 2, 256, group_size(t) * ROWS), BF16) for t in TARGETS]
    shapes += [
        vmem((LEVELS, WIDTH, WIDTH), BF16),
        vmem((LEVELS, CHIPS, PAIR, WIDTH), BF16),
        vmem((LEVELS, PAIR, WIDTH), BF16),
        vmem((LEVELS, PAIR, WIDTH), BF16),
        vmem((CHIPS, PAIR, WIDTH), BF16),
    ]
    shapes += [vmem((group_size(t) * PAIR, PART), F32) for t in TARGETS]
    shapes += [vmem((group_size(t), PAIR, PART), BF16) for t in TARGETS]
    shapes += [vmem((group_size(t), PAIR, PART), BF16) for t in TARGETS]
    shapes += [vmem((LEVELS, CHIPS, PAIR, PART), BF16)]
    shapes += [vmem((2, group_size(t), ROWS, PART), BF16) for t in TARGETS]
    shapes += [
        vmem((TOP, 2, 256, PART), F32),
        vmem((TOP, CHIPS, 2, ROWS, PART), BF16),
        vmem((TOP, CHIPS, 2, ROWS, PART), BF16),
        vmem((LEVELS, 2, ROWS, PART), F32),
        vmem((LEVELS, ROWS, COLUMNS), BF16),
        vmem((2, LEVELS, ROWS, PART), BF16),
        vmem((2, LEVELS, ROWS, PART), BF16),
        vmem((2 * LEVELS, 2, ROWS, PART), BF16),
        vmem((2 * LEVELS, ROWS, PART), BF16),
        vmem((ROWS, PART), F32),
        vmem((2, ROWS, PART), BF16),
        vmem((2 * LEVELS, ROWS, COLUMNS), BF16),
        pltpu.SMEM((LEVELS,), jnp.int32),
        pltpu.SMEM((1, 178), jnp.int32),
        pltpu.SemaphoreType.DMA((SLOTS,)),
        pltpu.SemaphoreType.DMA((SLOTS,)),
        pltpu.SemaphoreType.DMA((24,)),
        pltpu.SemaphoreType.DMA((3,)),
    ]
    return shapes


def deliver(a, b, a_out, b_out):
    a_out[...] = a[...]
    b_out[...] = b[...]


def shards(rhs, diag_inverse, factor, widths, structure):
    out = jax.ShapeDtypeStruct((LEVELS, 1, ROWS, COLUMNS), BF16)
    hbm = pl.BlockSpec(memory_space=pltpu.HBM)
    solved = pl.pallas_call(
        kernel,
        out_shape=(out, out),
        in_specs=[hbm] * 5,
        out_specs=[hbm] * 2,
        scratch_shapes=scratch_shapes(),
        compiler_params=pltpu.CompilerParams(
            collective_id=0, has_side_effects=True, vmem_limit_bytes=58 * 2**20
        ),
    )(rhs, diag_inverse, factor, widths.reshape(LEVELS), structure)
    vmem = pl.BlockSpec(memory_space=pltpu.VMEM)
    return pl.pallas_call(
        deliver,
        out_shape=(out, out),
        in_specs=[vmem] * 2,
        out_specs=[vmem] * 2,
    )(*solved)


def solution(mesh):
    placed = (
        P(None, "leaf", "row", None),
        P("leaf", None, None, None),
        P("leaf", None, "row", None),
        P(None, "leaf"),
        P("leaf", None),
    )
    return jax.shard_map(
        shards,
        mesh=mesh,
        in_specs=placed,
        out_specs=(P(None, "leaf", "row", None), P(None, "leaf", "row", None)),
        check_vma=False,
    )
```

```python
import jax
import jax.numpy as jnp
from jax import lax
from jax.experimental import pallas as pl
from jax.experimental.pallas import tpu as pltpu
from jax.sharding import PartitionSpec as P

MESH = pl.DeviceIdType.MESH
F32 = jnp.float32
BF16 = jnp.bfloat16
LEVELS = 6
LEAVES = 16
CHIPS = 8
ROWS = 32
PAIR = 2 * ROWS
WIDTH = 512
COLUMNS = 256
PART = COLUMNS // 2
TARGETS = tuple(range(1, LEVELS))
TOP = LEVELS - 1
Z_ORDER = (0, 1, 7, 2, 6, 3, 5, 4)
Z_SLOT = {d: i for i, d in enumerate(Z_ORDER)}
FAR_FIRST = Z_ORDER[:0:-1]


def group_size(level):
    return min(2**level, LEAVES)


def block_offsets():
    table, cursor = {}, 0
    for source in range(LEVELS):
        for target in range(source + 1, LEVELS):
            table[source, target] = cursor
            cursor += group_size(target)
    return table


OFFSETS = block_offsets()


def dot(a, b):
    return jnp.dot(a, b, preferred_element_type=F32)


def dot_nt(a, b):
    return lax.dot_general(a, b, (((1,), (1,)), ((), ())), preferred_element_type=F32)


ROW_Z, LEAF, B_LEAF, B_Z = (i * 2 * LEVELS for i in range(4))
FOLD, FOLD_T = 8 * LEVELS, 9 * LEVELS
RHS_X, FWD_X, HEAD_X = (10 * LEVELS + i for i in range(3))
SLOTS = 10 * LEVELS + 3


def ring(d, n):
    return min(d, n - d) if n > 2 else d


def extent(span):
    deep = min(span, 4)
    return span // deep, deep


def leaf_order(span):
    wide, deep = extent(span)
    steps = [(dx, dy) for dx in range(wide) for dy in range(deep)]
    return sorted(steps, key=lambda d: ring(d[0], wide) + ring(d[1], deep))


def leaf_back(span, step):
    wide, deep = extent(span)
    return leaf_order(span).index((-step[0] % wide, -step[1] % deep))


def kernel(rhs_hbm, diag, factor, widths_hbm, structure_hbm, fwd, adj, *scratch):
    scratch = list(scratch)

    def take(n):
        out = scratch[:n]
        del scratch[:n]
        return out

    per_target = lambda: dict(zip(TARGETS, take(len(TARGETS))))
    blocks, sorted_blocks, fold, fold_t = per_target(), per_target(), per_target(), per_target()
    dm, dm_t, own_rows, twice, turned = take(5)
    pre, part_out, part_in = per_target(), per_target(), per_target()
    (resid,) = take(1)
    gathered = per_target()
    pulled_pre, pair_out, pair_in, head = take(4)
    rhs, rhs_out, rhs_in, fwd_out, fwd_in, head_in, first_out, whole = take(8)
    widths, structure = take(2)
    send_sem, recv_sem, load_sem, out_sem = take(4)

    leaf = lax.axis_index("leaf")
    row = lax.axis_index("row")
    z, core = row // 2, lax.rem(row, 2)
    other = 1 - core
    sibling = z * 2 + other

    loads = {}

    def load(name, src, dst):
        loads[name] = pltpu.make_async_copy(src, dst, load_sem.at[len(loads)])
        loads[name].start()

    load("widths", widths_hbm, widths)
    load("rhs", rhs_hbm.at[:, 0], rhs)

    barrier = pltpu.get_barrier_semaphore()

    def greet(leaf_to, row_to):
        pl.semaphore_signal(barrier, inc=1, device_id=(leaf_to, row_to), device_id_type=MESH)

    for k in FAR_FIRST:
        for c in range(2):
            greet(leaf, lax.rem(z + k, CHIPS) * 2 + c)
    for k in range(1, LEAVES):
        greet(lax.rem(leaf + k, LEAVES), row)
    greet(leaf, sibling)

    load("structure", structure_hbm, structure)
    load("diag", diag.at[0], dm)
    for t in TARGETS:
        for s in range(t):
            load((s, t), factor.at[0, pl.ds(OFFSETS[s, t], group_size(t))], blocks[t].at[s])

    sends = []

    def send(src, dst, slot, leaf_to, row_to):
        pltpu.make_async_remote_copy(
            src_ref=src,
            dst_ref=dst,
            send_sem=send_sem.at[slot],
            recv_sem=recv_sem.at[slot],
            device_id=(leaf_to, row_to),
            device_id_type=MESH,
        ).start()

    def wait(sem, slot, ref):
        pltpu.make_async_copy(ref, ref, sem.at[slot]).wait()

    def drain():
        for slot, ref in sends:
            wait(send_sem, slot, ref)
        sends.clear()

    def receive(slot, ref):
        wait(recv_sem, slot, ref)
        sends.append((slot, ref))

    def member(span, step):
        wide, deep = extent(span)
        me = lax.rem(leaf, span)
        x = lax.rem(me // deep + step[0], wide)
        return x * deep + lax.rem(lax.rem(me, deep) + step[1], deep)

    def leaf_of(span, step):
        return leaf // span * span + member(span, step)

    def row_mask(level, first, count):
        rows = first + lax.broadcasted_iota(jnp.int32, (count, 1), 0)
        return (rows < widths[level]).astype(F32)

    def pair_mask(level):
        return row_mask(level, z * PAIR, PAIR)

    def prepare_diag(s):
        masked = (dm[s].astype(F32) * row_mask(s, 0, WIDTH)).astype(BF16)
        turned[...] = masked.T.reshape(CHIPS, PAIR, WIDTH)
        for i, d in enumerate(Z_ORDER):
            dm_t[s, i] = turned[lax.rem(z + d, CHIPS)]
        everything = dm_t[s].reshape(WIDTH, WIDTH)
        twice[s] = dot_nt(dm_t[s, 0], everything).astype(BF16)
        wanted = z * PAIR + lax.broadcasted_iota(jnp.int32, (PAIR, WIDTH), 0)
        at = lax.broadcasted_iota(jnp.int32, (PAIR, WIDTH), 1)
        chosen = (at == wanted).astype(F32).astype(BF16)
        own_rows[s] = dot_nt(chosen, everything).astype(BF16)

    def sort_blocks(t):
        for s in range(t):
            loads[s, t].wait()
        span = group_size(t)

        def scale(s, carry):
            first = OFFSETS[0, t]
            for later in range(1, t):
                first = jnp.where(s == later, OFFSETS[later, t], first)
            for i, step in enumerate(leaf_order(span)):
                p = member(span, step)
                w = structure[0, first + p].astype(F32)
                sorted_blocks[t][s, i] = (blocks[t][s, p].astype(F32) * w).astype(BF16)
            return carry

        lax.fori_loop(0, t, scale, 0)

    def prepare_fold(t):
        sort_blocks(t)
        span = group_size(t)

        def step(s, carry):
            flat = sorted_blocks[t][s].reshape(span * ROWS, WIDTH)
            for k in range(2):
                part = dot_nt(flat, dm_t[s, pl.ds(k * 4, 4)].reshape(256, WIDTH)).astype(BF16)
                fold[t][s, :, core, :, k * 256 : (k + 1) * 256] = part.reshape(span, ROWS, 256)
            return carry

        lax.fori_loop(0, t, step, 0)
        mine = fold[t].at[:, :, core]
        send(mine, mine, FOLD + t, leaf, sibling)

    def prepare_fold_t(t):
        height = group_size(t) * ROWS

        def step(s, carry):
            flat = sorted_blocks[t][s].reshape(height, WIDTH)
            for m in range(2):
                part = dot_nt(dm_t[s, pl.ds(m * 4, 4)].reshape(256, WIDTH), flat)
                fold_t[t][s, core, m] = part.astype(BF16)
            return carry

        lax.fori_loop(0, t, step, 0)
        mine = fold_t[t].at[:, core]
        send(mine, mine, FOLD_T + t, leaf, sibling)

    def prepare_third():
        prepare_diag(2)
        prepare_fold(3)

    def full(level):
        return resid[level].reshape(WIDTH, PART)

    def prepare_pre(t):
        receive(FOLD + t, fold[t].at[:, :, 0])
        height = group_size(t) * PAIR
        total = None
        for s in range(t - 1):
            term = dot(fold[t][s].reshape(height, WIDTH), full(s))
            total = term if total is None else total + term
        if total is not None:
            pre[t][...] = total

    def outputs(level):
        fwd_out[level] = dot(own_rows[level], full(level)).astype(BF16).reshape(2, ROWS, PART)
        head[level] = dot(twice[level], full(level)).reshape(2, ROWS, PART)

    def prepare_pulled(s):
        for m in range(2):
            total = None
            for t in range(s + 2, LEVELS):
                for b in range(2):
                    values = gathered[t][b].reshape(group_size(t) * ROWS, PART)
                    term = dot(fold_t[t][s, b, m], values)
                    total = term if total is None else total + term
            pulled_pre[s, m] = total

    def send_gathered(level, block):
        span = group_size(level)
        gathered[level][:, 0] = block
        for step in reversed(leaf_order(span)[1:]):
            there = leaf_back(span, step)
            send(
                gathered[level].at[:, 0],
                gathered[level].at[:, there],
                B_LEAF + 2 * level + (2 * there >= span),
                leaf_of(span, step),
                row,
            )

    loads["widths"].wait()
    loads["rhs"].wait()
    first = (rhs[0].astype(F32) * row_mask(0, row * ROWS, ROWS)).astype(BF16)
    for c in range(2):
        first_out[c] = first[:, c * PART : (c + 1) * PART]
        rhs_out[c] = rhs[:, :, c * PART : (c + 1) * PART]
    mine = pl.ds(pl.multiple_of(core * ROWS, ROWS), ROWS)
    resid[0, 0, mine] = first_out[core]
    pl.semaphore_wait(barrier, LEAVES + 14)
    for d in FAR_FIRST:
        there = resid.at[0, Z_SLOT[-d % CHIPS], mine]
        for c in range(2):
            to = lax.rem(z + d, CHIPS) * 2 + c
            send(first_out.at[c], there, ROW_Z + (Z_SLOT[-d % CHIPS] > 3), leaf, to)
    send(first_out.at[other], resid.at[0, 0, mine], ROW_Z, leaf, sibling)
    send(rhs_out.at[other], rhs_in.at[core], RHS_X, leaf, sibling)
    rhs_in[core] = rhs_out[core]

    for level in range(LEVELS):
        if level > 0:
            span = group_size(level)
            near = span // 2
            value = rhs_in[:, level].reshape(PAIR, PART).astype(F32)
            if near > 1:
                receive(LEAF + 2 * level, part_in[level].at[pl.ds(0, near - 1)])
            value = value - jnp.sum(part_in[level][:near].astype(F32), axis=0)
            receive(LEAF + 2 * level + 1, part_in[level].at[pl.ds(0, near)])
            value = value - jnp.sum(part_in[level][near:].astype(F32), axis=0)
            resid[level, 0] = (value * pair_mask(level)).astype(BF16)
            for d in FAR_FIRST:
                there = Z_SLOT[-d % CHIPS]
                send(
                    resid.at[level, 0],
                    resid.at[level, there],
                    ROW_Z + 2 * level + (there > 3),
                    leaf,
                    lax.rem(z + d, CHIPS) * 2 + core,
                )
        if level == 0:
            loads["diag"].wait()
            loads["structure"].wait()
            prepare_diag(0)
            prepare_fold(1)
            prepare_diag(1)
            prepare_fold(2)
        elif level == 1:
            prepare_diag(3)
            prepare_fold(4)
        elif level == 2:
            prepare_fold(5)
        elif level == 3:
            prepare_fold_t(4)
        elif level == 4:
            prepare_fold_t(3)
        else:
            outputs(4)
            send(head.at[0, other], head_in, HEAD_X, leaf, sibling)
        target = level + 1
        if level < TOP:
            prepare_pre(target)
            span = group_size(target)
            near = span // 2
            height = near * PAIR
        for k in range(2):
            if level > 0:
                receive(ROW_Z + 2 * level + k, resid.at[level, pl.ds(0, 3 + k)])
            elif k:
                receive(ROW_Z + 1, resid.at[pl.ds(0, 4), pl.ds(0, 2), pl.ds(0, ROWS)])
            else:
                receive(ROW_Z, resid.at[0, pl.ds(0, 7), pl.ds(0, ROWS)])
            if level == TOP:
                continue
            if level == 0 and k:
                pl.when(core == 1)(prepare_third)
            values = resid[level, k * 4 : k * 4 + 4].reshape(256, PART)
            for m in (1, 0):
                rows = slice(m * height, (m + 1) * height)
                half = fold[target][level, m * near : (m + 1) * near]
                half = half.reshape(height, WIDTH)[:, k * 256 : (k + 1) * 256]
                total = dot(half, values)
                if target > 1 or k:
                    total = total + pre[target][rows]
                if k == 0:
                    pre[target][rows] = total
                    continue
                total = total.astype(BF16).reshape(near, PAIR, PART)
                part_out[target][m * near : (m + 1) * near] = total
                for i in reversed(range(max(m * near, 1), (m + 1) * near)):
                    step = leaf_order(span)[i]
                    there = leaf_back(span, step)
                    send(
                        part_out[target].at[i],
                        part_in[target].at[there],
                        LEAF + 2 * target + (there >= near),
                        leaf_of(span, step),
                        row,
                    )
                if m == 0:
                    part_in[target][0] = part_out[target][0]
        if level == 0:
            pl.when(core == 0)(prepare_third)
            receive(RHS_X, rhs_in.at[0])
        elif level == 1:
            prepare_diag(4)
            prepare_fold_t(1)
        elif level == 2:
            prepare_diag(5)
            outputs(0)
            outputs(1)
        elif level == 3:
            outputs(2)
            prepare_fold_t(5)
        elif level == 4:
            outputs(3)
            prepare_fold_t(2)
    solved = dot(twice[TOP], full(TOP))
    block = (solved * pair_mask(TOP)).astype(BF16).reshape(2, ROWS, PART)
    adj_out = fwd_out.at[pl.ds(LEVELS, LEVELS)]
    adj_out[0] = jnp.zeros((2, ROWS, PART), BF16)
    adj_out[TOP] = block
    send_gathered(TOP, block)
    for level in reversed(range(TOP)):
        upper = level + 1
        span = group_size(upper)
        near = span // 2
        if level == TOP - 1:
            outputs(TOP)
            for t in reversed(TARGETS):
                receive(FOLD_T + t, fold_t[t].at[:, 0])
        begun = upper < TOP
        for k in range(2):
            if k:
                receive(B_LEAF + 2 * upper + 1, gathered[upper].at[:, pl.ds(0, near)])
            elif near > 1:
                receive(B_LEAF + 2 * upper, gathered[upper].at[:, pl.ds(0, near - 1)])
            if span >= 8:
                first, count = k * near, near
            elif k:
                first, count = 0, span
            else:
                continue
            for m in (1, 0):
                total = None
                for b in range(2):
                    values = gathered[upper][b, first : first + count]
                    half = fold_t[upper][
                        level, b, m, :, first * ROWS : (first + count) * ROWS
                    ]
                    term = dot(half, values.reshape(count * ROWS, PART))
                    total = term if total is None else total + term
                if begun:
                    total = total + pulled_pre[level, m]
                if k == 0:
                    pulled_pre[level, m] = total
                    continue
                pair_out[level, m * 4 : m * 4 + 4] = total.astype(BF16).reshape(4, 2, ROWS, PART)
                for d in reversed(Z_ORDER[max(m * 4, 1) : m * 4 + 4]):
                    i, there = Z_SLOT[d], Z_SLOT[-d % CHIPS]
                    to = lax.rem(z + d, CHIPS)
                    slot = B_Z + 2 * level + (there > 3)
                    if level > 0:
                        send(
                            pair_out.at[level, i],
                            pair_in.at[level, there],
                            slot,
                            leaf,
                            to * 2 + core,
                        )
                        continue
                    for b in range(2):
                        landing = pair_in.at[0, there, core]
                        send(pair_out.at[0, i, b], landing, slot, leaf, to * 2 + b)
            begun = True
        if level > 0:
            pair_in[level, 0] = pair_out[level, 0]
            prepare_pulled(level - 1)
            value = head[level]
            receive(B_Z + 2 * level, pair_in.at[level, pl.ds(0, 3)])
            value = value - jnp.sum(pair_in[level, :4].astype(F32), axis=0)
            receive(B_Z + 2 * level + 1, pair_in.at[level, pl.ds(0, 4)])
            value = value - jnp.sum(pair_in[level, 4:].astype(F32), axis=0)
            block = (value * pair_mask(level).reshape(2, ROWS, 1)).astype(BF16)
            adj_out[level] = block
            send_gathered(level, block)
            if level == 1:
                send(fwd_out.at[:, other], fwd_in, FWD_X, leaf, sibling)
                receive(HEAD_X, head_in)
            continue
        send(pair_out.at[0, 0, other], pair_in.at[0, 0, core], B_Z, leaf, sibling)
        pair_in[0, 0, core] = pair_out[0, 0, core]
        receive(FWD_X, fwd_in)
        for i in range(2 * LEVELS):
            if i == LEVELS:
                continue
            for c in range(2):
                block = jnp.where(core == c, fwd_out[i, core], fwd_in[i])
                whole[i, :, c * PART : (c + 1) * PART] = block
        stores = [
            (whole.at[pl.ds(0, LEVELS)], fwd.at[:, 0]),
            (whole.at[pl.ds(LEVELS + 1, TOP)], adj.at[pl.ds(1, TOP), 0]),
            (whole.at[LEVELS], adj.at[0, 0]),
        ]
        stores = [pltpu.make_async_copy(*pair, out_sem.at[i]) for i, pair in enumerate(stores)]
        stores[0].start()
        stores[1].start()
        drain()
        receive(B_Z, pair_in.at[0, pl.ds(0, 7), 0])
        near_sum = jnp.sum(pair_in[0, :4].astype(F32), axis=0)
        receive(B_Z + 1, pair_in.at[0, pl.ds(0, 4)])
        pulled = near_sum + jnp.sum(pair_in[0, 4:].astype(F32), axis=0)
        mask = row_mask(0, row * ROWS, ROWS)
        for c in range(2):
            ahead = jnp.where(core == c, head[0, core], head_in[...])
            block = ((ahead - pulled[c]) * mask).astype(BF16)
            whole[LEVELS, :, c * PART : (c + 1) * PART] = block
        stores[2].start()
        drain()
        for store in stores:
            store.wait()


def scratch_shapes():
    vmem = pltpu.VMEM
    shapes = []
    for _ in range(2):
        shapes += [vmem((t, group_size(t), ROWS, WIDTH), BF16) for t in TARGETS]
    shapes += [vmem((t, group_size(t), 2, ROWS, WIDTH), BF16) for t in TARGETS]
    shapes += [vmem((t, 2, 2, 256, group_size(t) * ROWS), BF16) for t in TARGETS]
    shapes += [
        vmem((LEVELS, WIDTH, WIDTH), BF16),
        vmem((LEVELS, CHIPS, PAIR, WIDTH), BF16),
        vmem((LEVELS, PAIR, WIDTH), BF16),
        vmem((LEVELS, PAIR, WIDTH), BF16),
        vmem((CHIPS, PAIR, WIDTH), BF16),
    ]
    shapes += [vmem((group_size(t) * PAIR, PART), F32) for t in TARGETS]
    shapes += [vmem((group_size(t), PAIR, PART), BF16) for t in TARGETS]
    shapes += [vmem((group_size(t), PAIR, PART), BF16) for t in TARGETS]
    shapes += [vmem((LEVELS, CHIPS, PAIR, PART), BF16)]
    shapes += [vmem((2, group_size(t), ROWS, PART), BF16) for t in TARGETS]
    shapes += [
        vmem((TOP, 2, 256, PART), F32),
        vmem((TOP, CHIPS, 2, ROWS, PART), BF16),
        vmem((TOP, CHIPS, 2, ROWS, PART), BF16),
        vmem((LEVELS, 2, ROWS, PART), F32),
        vmem((LEVELS, ROWS, COLUMNS), BF16),
        vmem((2, LEVELS, ROWS, PART), BF16),
        vmem((2, LEVELS, ROWS, PART), BF16),
        vmem((2 * LEVELS, 2, ROWS, PART), BF16),
        vmem((2 * LEVELS, ROWS, PART), BF16),
        vmem((ROWS, PART), F32),
        vmem((2, ROWS, PART), BF16),
        vmem((2 * LEVELS, ROWS, COLUMNS), BF16),
        pltpu.SMEM((LEVELS,), jnp.int32),
        pltpu.SMEM((1, 178), jnp.int32),
        pltpu.SemaphoreType.DMA((SLOTS,)),
        pltpu.SemaphoreType.DMA((SLOTS,)),
        pltpu.SemaphoreType.DMA((24,)),
        pltpu.SemaphoreType.DMA((3,)),
    ]
    return shapes


def deliver(a, b, a_out, b_out):
    a_out[...] = a[...]
    b_out[...] = b[...]


def shards(rhs, diag_inverse, factor, widths, structure):
    out = jax.ShapeDtypeStruct((LEVELS, 1, ROWS, COLUMNS), BF16)
    hbm = pl.BlockSpec(memory_space=pltpu.HBM)
    solved = pl.pallas_call(
        kernel,
        out_shape=(out, out),
        in_specs=[hbm] * 5,
        out_specs=[hbm] * 2,
        scratch_shapes=scratch_shapes(),
        compiler_params=pltpu.CompilerParams(
            collective_id=0, has_side_effects=True, vmem_limit_bytes=58 * 2**20
        ),
    )(rhs, diag_inverse, factor, widths.reshape(LEVELS), structure)
    vmem = pl.BlockSpec(memory_space=pltpu.VMEM)
    return pl.pallas_call(
        deliver,
        out_shape=(out, out),
        in_specs=[vmem] * 2,
        out_specs=[vmem] * 2,
    )(*solved)


def solution(mesh):
    placed = (
        P(None, "leaf", "row", None),
        P("leaf", None, None, None),
        P("leaf", None, "row", None),
        P(None, "leaf"),
        P("leaf", None),
    )
    return jax.shard_map(
        shards,
        mesh=mesh,
        in_specs=placed,
        out_specs=(P(None, "leaf", "row", None), P(None, "leaf", "row", None)),
        check_vma=False,
    )
```
